512 devices in a mesh: kvh: 8 (over x, core), ctx: 64 (over y, z).
Axes of the slice: x: 4, y: 8, z: 8, core: 2. Of those that a mesh axis runs over, the one named last changes fastest.
Arguments:
- queries: bfloat16 [128, 8192], P(None, 'kvh'), may hold values from -130 to 130
- cache_keys: bfloat16 [65536, 1024], P('ctx', 'kvh'), may hold values from -6 to 6
- cache_values: bfloat16 [65536, 1024], P('ctx', 'kvh'), may hold values from -6 to 6
- lengths: int32 [64], P('ctx'), may hold values from 2 to 1024, as said below
- w_out: bfloat16 [8192, 8192], P('kvh', 'ctx'), may hold values from -0.0625 to 0.0625
Outputs:
- mixed: bfloat16 [128, 8192], P('kvh', 'ctx')
The draws below stay inside these ranges and needn't reach their ends.
Inputs may be any that keep to these rules, and one draw needn't show every extreme that they name: `lengths`: the number of valid positions at the start of each segment of 1024 positions; at least one segment is full.
All inputs are finite; a program needn't handle non-finite values.
Results may differ from the reference program's by a relative error of at most 0.005.
Values may be sent and summed in bfloat16 or wider, within the bound.
A program may use at most 192 MiB of HBM per device.

```python
import math
import jax
import jax.numpy as jnp
from jax import lax

HEADS = 64
KVH = 8
HD = 128
D = 8192
QROWS = 128
CTX_DEV = 1024
CONTEXT = 65536


def key_table(key):
    return jnp.clip(jax.random.normal(key, (CONTEXT, KVH * HD), jnp.float32), -6.0, 6.0)


def draw_cache_keys(key, part):
    table = key_table(key)
    return table.astype(jnp.bfloat16)


def draw_queries(key, part):
    key = jax.random.fold_in(key, 5)
    values = jnp.clip(3.5 * jax.random.normal(key, (QROWS, HEADS * HD), jnp.float32), -21.0, 21.0)
    return values.astype(jnp.bfloat16)


def draw_lengths(key, part):
    key = jax.random.fold_in(key, 9)
    first_key, second_key = jax.random.split(key)
    segment_count = CONTEXT // CTX_DEV
    counts = jax.random.randint(first_key, (segment_count,), 2, CTX_DEV + 1, dtype=jnp.int32)
    chosen = jax.random.randint(second_key, (), 0, segment_count, dtype=jnp.int32)
    return jnp.where(jnp.arange(segment_count, dtype=jnp.int32) == chosen, CTX_DEV, counts).astype(jnp.int32)


def shard_levels(key, extent, pieces, low, high):
    gain, own = 1.0, jax.random.fold_in(key, 6)
    for position, blocks in pieces:
        draws = jnp.exp(jax.random.uniform(jax.random.fold_in(own, position), (blocks,), jnp.float32, low / len(pieces), high / len(pieces)))
        gain = gain * jnp.repeat(draws, extent[position] // blocks).reshape([-1 if axis == position else 1 for axis in range(len(extent))])
    return gain


def scatter_about(own_key, shape, width, bound, cuts=(), held_as=jnp.bfloat16):
    result = jax.random.normal(own_key, shape, jnp.float32) * width
    if len(cuts) > 0:
        result = shard_levels(own_key, shape, cuts, -0.22, 0.18) * result
    return jnp.clip(result, min=-bound, max=bound).astype(held_as)


def setup_inputs(seed: int = 0) -> dict:
    key_list = jax.random.split(jax.random.key(seed), 6)
    queries = draw_queries(jax.random.fold_in(key_list[5], 71), 0)
    cache_keys = draw_cache_keys(jax.random.fold_in(key_list[5], 71), 0)
    cache_values = scatter_about(key_list[2], (CONTEXT, KVH * HD), 1.0, 6.0, ((0, 64), (1, 8)))
    lengths = draw_lengths(jax.random.fold_in(key_list[5], 71), 0)
    w_out = scatter_about(key_list[4], (D, D), D ** -0.5, 0.0625, ((0, 8), (1, 64)))
    return {"queries": queries, "cache_keys": cache_keys, "cache_values": cache_values, "lengths": lengths, "w_out": w_out}


def segment_partials(query_group, key_slab, value_slab, valid_count):
    score_scale = 1.0 / math.sqrt(HD)
    scores = jnp.einsum('qhd,kd->hqk', query_group.astype(jnp.float32), key_slab.astype(jnp.float32)) * score_scale
    valid_mask = jnp.arange(key_slab.shape[0], dtype=jnp.int32) < valid_count
    scores = jnp.where(valid_mask[None, None, :], scores, -jnp.inf)
    seg_max = lax.optimization_barrier(jnp.max(scores, axis=-1))
    weights = jnp.exp(scores - seg_max[:, :, None])
    seg_total = lax.optimization_barrier(jnp.sum(weights, axis=-1))
    rounded_weights = weights.astype(jnp.bfloat16).astype(jnp.float32)
    seg_out = jnp.einsum('hqk,kd->qhd', rounded_weights, value_slab.astype(jnp.float32))
    return (seg_max, seg_total, seg_out)

def reference(queries, cache_keys, cache_values, lengths, w_out):
    per_group = HEADS // KVH
    segment_count = CONTEXT // CTX_DEV
    attended_list = []
    for group_index in range(KVH):
        key_slabs = cache_keys[:, group_index * HD:(group_index + 1) * HD].reshape(segment_count, CTX_DEV, HD)
        value_slabs = cache_values[:, group_index * HD:(group_index + 1) * HD].reshape(segment_count, CTX_DEV, HD)
        query_group = queries[:, group_index * per_group * HD:(group_index + 1) * per_group * HD].reshape(QROWS, per_group, HD)

        def one_segment(operands):
            return segment_partials(query_group, operands[0], operands[1], operands[2])
        seg_max, seg_total, seg_out = lax.map(one_segment, (key_slabs, value_slabs, lengths))
        peak = lax.optimization_barrier(jnp.max(seg_max, axis=0))
        factor = jnp.exp(seg_max - peak[None])
        total = lax.optimization_barrier(jnp.sum(factor * seg_total, axis=0))
        numer = lax.optimization_barrier(jnp.sum(seg_out * jnp.transpose(factor, (0, 2, 1))[:, :, :, None], axis=0))
        attended_list.append((numer / total.T[:, :, None]).reshape(QROWS, per_group * HD))
    attended = jnp.concatenate(attended_list, axis=1).astype(jnp.bfloat16)
    return jnp.dot(attended, w_out, preferred_element_type=jnp.float32).astype(jnp.bfloat16)
```

```python
import functools
import math

import jax
import jax.numpy as jnp
from jax import lax
from jax.experimental import pallas as pl
from jax.experimental.pallas import tpu as pltpu
from jax.sharding import PartitionSpec as P

HD = 128
HALF = HD // 2
STAT_ROWS = 16
MASKED = -1e30
SCALE = 1.0 / math.sqrt(HD)
LOG2E = math.log2(math.e)
MESH = pl.DeviceIdType.MESH


def ceil_to(value, unit):
    return -(-value // unit) * unit


def split_rows(stat, rows):
    high = stat.astype(jnp.bfloat16).astype(jnp.float32)
    rest = stat - high
    middle = rest.astype(jnp.bfloat16).astype(jnp.float32)
    low = rest - middle
    row = lax.broadcasted_iota(jnp.int32, (rows, stat.shape[1]), 0)
    return jnp.where(
        row == 0, high, jnp.where(row == 1, middle, jnp.where(row == 2, low, 0.0))
    )


def join_rows(rows):
    return rows[0:1] + rows[1:2] + rows[2:3]


def merge(parts, stats):
    top = functools.reduce(jnp.maximum, stats)
    shares = [jnp.exp(stat - top) for stat in stats]
    total = functools.reduce(jnp.add, shares)
    merged = functools.reduce(
        jnp.add, [part * share for part, share in zip(parts, shares)]
    )
    return merged / total, top + jnp.log(total)


def kernel(
    nk, n,
    len_hbm, q_hbm, k_hbm, v_hbm, w_hbm, out_ref,
    len_ref, q_ref, k_ref, v_ref, w_ref, vt_ref, wt_ref,
    send1, recv1, send2, recv2, att, send3, recv3,
    load_sem, send_sem, recv_sem,
):
    rows = q_ref.shape[0]
    keys = k_ref.shape[0]
    share = HALF // n
    kvh = lax.axis_index("kvh")
    ctx = lax.axis_index("ctx")
    y, z = ctx // n, lax.rem(ctx, n)

    loads = [
        pltpu.make_async_copy(q_hbm, q_ref, load_sem.at[0]),
        pltpu.make_async_copy(k_hbm, k_ref.at[:, pl.ds(0, HD)], load_sem.at[1]),
        pltpu.make_async_copy(v_hbm, v_ref, load_sem.at[2]),
        pltpu.make_async_copy(w_hbm, w_ref, load_sem.at[3]),
        pltpu.make_async_copy(len_hbm, len_ref, load_sem.at[4]),
    ]
    for load in loads:
        load.start()

    def on_y(step):
        return (kvh, lax.rem(y + step, n) * n + z)

    def on_z(step):
        return (kvh, y * n + lax.rem(z + step, n))

    def on_kvh(step):
        return (lax.rem(kvh + step, nk), ctx)

    barrier = pltpu.get_barrier_semaphore()
    for step in range(1, n):
        pl.semaphore_signal(barrier, inc=1, device_id=on_y(step), device_id_type=MESH)
        pl.semaphore_signal(barrier, inc=1, device_id=on_z(step), device_id_type=MESH)
    for step in range(1, nk):
        pl.semaphore_signal(barrier, inc=1, device_id=on_kvh(step), device_id_type=MESH)

    def send(src, dst, index, device):
        pltpu.make_async_remote_copy(
            src_ref=src, dst_ref=dst, send_sem=send_sem.at[index],
            recv_sem=recv_sem.at[index], device_id=device, device_id_type=MESH,
        ).start()

    def take(ref, sem):
        pltpu.make_async_copy(ref, ref, sem).wait()

    loads[4].wait()
    position = lax.broadcasted_iota(jnp.int32, (keys, HD), 0)
    column = lax.broadcasted_iota(jnp.int32, (keys, HD), 1)
    bias = jnp.where((column == 0) & (position >= len_ref[0]), MASKED, 0.0)
    k_ref[:, HD:] = bias.astype(jnp.bfloat16)
    lane = lax.broadcasted_iota(jnp.int32, (2 * rows, HD), 1)
    unit = jnp.where(lane == 0, 1.0, 0.0).astype(jnp.bfloat16)

    loads[2].wait()
    vt_ref[:HD] = v_ref[...].T
    vt_ref[HD:] = jnp.ones((STAT_ROWS, keys), jnp.bfloat16)
    loads[0].wait()
    loads[1].wait()
    pl.semaphore_wait(barrier, 2 * (n - 1) + nk - 1)

    for pair in range(n // 2):
        heads = [lax.rem(y + 1 + 2 * pair, n), lax.rem(y + 2 + 2 * pair, n)]
        query = jnp.concatenate(
            [q_ref[:, pl.ds(pl.multiple_of(h * HD, HD), HD)] for h in heads], axis=0
        )
        query = jnp.concatenate([query, unit], axis=1)
        scores = lax.dot_general(
            k_ref[...], query, (((1,), (1,)), ((), ())),
            preferred_element_type=jnp.float32,
        )
        peak = jnp.max(scores, axis=0, keepdims=True)
        weights = jnp.exp2((scores - peak) * (SCALE * LOG2E)).astype(jnp.bfloat16)
        outs = jnp.dot(vt_ref[...], weights, preferred_element_type=jnp.float32)
        total = outs[HD : HD + 1]
        stat = peak * SCALE + jnp.log(total)
        outs = (outs[:HD] / total).astype(jnp.bfloat16)
        tail = split_rows(stat, STAT_ROWS).astype(jnp.bfloat16)
        for slot, h in enumerate(heads):
            here = slice(slot * rows, (slot + 1) * rows)
            own = pair == n // 2 - 1 and slot == 1
            first = recv1.at[0, y] if own else send1.at[0, h]
            first[:HALF] = outs[:HALF, here]
            first[HALF:] = tail[:, here]
            if not own:
                send(first, recv1.at[0, y], 0, (kvh, h * n + z))
            second = send1.at[1, h]
            second[:HALF] = outs[HALF:, here]
            second[HALF:] = tail[:, here]

            @pl.when(h != z)
            def _():
                send(second, recv1.at[1, z], 1, (kvh, y * n + h))

            @pl.when(h == z)
            def _():
                recv1[1, z, :HALF] = outs[HALF:, here]
                recv1[1, z, HALF:] = tail[:, here]

    loads[3].wait()
    for kind in range(2):
        for major in range(n):
            blocks = []
            for minor in range(n // 2):
                other = 2 * minor + (major + kind) % 2
                by, bz = (major, other) if kind == 0 else (other, major)
                for start in (by * HD + bz * share, bz * HD + HALF + by * share):
                    blocks.append(w_ref[start : start + share].astype(jnp.float32))
            block = jnp.concatenate(blocks, axis=0)
            at = (kind * n + major) * HALF
            wt_ref[:, at : at + HALF] = block.T.astype(jnp.bfloat16)

    message = send2.shape[2]
    mine = (y, z)
    for kind in range(2):
        take(recv1.at[kind, pl.ds(0, n - 1)], recv_sem.at[kind])
        merged, stat = merge(
            [recv1[kind, j, :HALF].astype(jnp.float32) for j in range(n)],
            [join_rows(recv1[kind, j, HALF:].astype(jnp.float32)) for j in range(n)],
        )
        tail = split_rows(stat, message - share)
        for j in range(n):
            piece = jnp.concatenate([merged[j * share : (j + 1) * share], tail], axis=0)
            send2[kind, j] = piece.astype(jnp.bfloat16)
        across = mine[1 - kind]
        recv2[kind, across] = send2[kind, across]
        for step in range(1, n):
            to = lax.rem(across + step, n)
            device = (kvh, y * n + to) if kind == 0 else (kvh, to * n + z)
            send(send2.at[kind, to], recv2.at[kind, across], 2 + kind, device)

    pieces = []
    for kind in range(2):
        take(recv2.at[kind, pl.ds(0, n - 1)], recv_sem.at[2 + kind])
        merged, _ = merge(
            [recv2[kind, j, :share].astype(jnp.float32) for j in range(n)],
            [
                join_rows(recv2[kind, j, share:].astype(jnp.float32))
                for j in range(n)
            ],
        )
        pieces.append(merged)
    parity = lax.rem(y + z, 2)
    major = y + parity * (z - y)
    minor = (z + parity * (y - z)) // 2
    att[parity, major, minor] = jnp.concatenate(pieces, axis=0).astype(jnp.bfloat16)

    for step in range(1, n):
        to = lax.rem(y + parity * step, n) * n + lax.rem(z + (1 - parity) * step, n)
        tile = att.at[parity, major, minor]
        send(tile, tile, 4, (kvh, to))
    tiles = att.at[0, pl.ds(0, n - 1), 0]
    take(tiles, recv_sem.at[4])
    for step in range(1, n):
        send(att.at[0, y], att.at[0, y], 5, on_y(step))
        send(att.at[1, z], att.at[1, z], 6, on_z(step))
    take(att.at[0, pl.ds(0, n - 1)], recv_sem.at[5])
    take(att.at[1, pl.ds(0, n - 1)], recv_sem.at[6])

    features = att[...].reshape(n * HD, rows)
    mixed = jnp.dot(wt_ref[...], features, preferred_element_type=jnp.float32).T
    send3[...] = mixed.reshape(send3.shape)
    for step in range(1, nk):
        to = lax.rem(kvh + step, nk)
        send(send3.at[to], recv3.at[kvh], 7, on_kvh(step))
    recv3[kvh] = send3[kvh]
    take(recv3.at[pl.ds(0, nk - 1)], recv_sem.at[7])
    out_ref[...] = jnp.sum(recv3[...], axis=0).astype(jnp.bfloat16)

    for kind in range(2):
        take(send1.at[kind, pl.ds(0, n - 1)], send_sem.at[kind])
        take(send2.at[kind, pl.ds(0, n - 1)], send_sem.at[2 + kind])
        take(att.at[kind, pl.ds(0, n - 1)], send_sem.at[5 + kind])
    take(tiles, send_sem.at[4])
    take(send3.at[pl.ds(0, nk - 1)], send_sem.at[7])


def solution(mesh):
    nk = mesh.shape["kvh"]
    n = math.isqrt(mesh.shape["ctx"])
    share = HALF // n
    message = ceil_to(share + 3, 16)

    def step(queries, cache_keys, cache_values, lengths, w_out):
        rows, keys = queries.shape[0], cache_keys.shape[0]
        bf16, f32 = jnp.bfloat16, jnp.float32
        anywhere = pl.BlockSpec(memory_space=pl.ANY)
        return pl.pallas_call(
            functools.partial(kernel, nk, n),
            out_shape=jax.ShapeDtypeStruct((rows // nk, HD), bf16),
            in_specs=[anywhere] * 5,
            out_specs=pl.BlockSpec(memory_space=pltpu.VMEM),
            scratch_shapes=[
                pltpu.SMEM((1,), jnp.int32),
                pltpu.VMEM(queries.shape, bf16),
                pltpu.VMEM((keys, 2 * HD), bf16),
                pltpu.VMEM((keys, HD), bf16),
                pltpu.VMEM(w_out.shape, bf16),
                pltpu.VMEM((HD + STAT_ROWS, keys), bf16),
                pltpu.VMEM((HD, n * HD), bf16),
                pltpu.VMEM((2, n, HALF + STAT_ROWS, rows), bf16),
                pltpu.VMEM((2, n, HALF + STAT_ROWS, rows), bf16),
                pltpu.VMEM((2, n, message, rows), bf16),
                pltpu.VMEM((2, n, message, rows), bf16),
                pltpu.VMEM((2, n, n // 2, 2 * share, rows), bf16),
                pltpu.VMEM((nk, rows // nk, HD), f32),
                pltpu.VMEM((nk, rows // nk, HD), f32),
                pltpu.SemaphoreType.DMA((5,)),
                pltpu.SemaphoreType.DMA((8,)),
                pltpu.SemaphoreType.DMA((8,)),
            ],
            compiler_params=pltpu.CompilerParams(
                collective_id=0, has_side_effects=True, vmem_limit_bytes=60 * 2**20
            ),
        )(lengths, queries, cache_keys, cache_values, w_out)

    in_specs = (P(None, "kvh"), P("ctx", "kvh"), P("ctx", "kvh"), P("ctx"), P("kvh", "ctx"))
    out_specs = P("kvh", "ctx")
    return jax.shard_map(step, mesh=mesh, in_specs=in_specs, out_specs=out_specs, check_vma=False)
```

```python
import functools
import math

import jax
import jax.numpy as jnp
from jax import lax
from jax.experimental import pallas as pl
from jax.experimental.pallas import tpu as pltpu
from jax.sharding import PartitionSpec as P

HD = 128
HALF = HD // 2
ONE_ROWS = 16
VMEM_BYTES = 53 * 2**20 + 800 * 2**10
MASKED = -1e30
SCALE = 1.0 / math.sqrt(HD)
LOG2E = math.log2(math.e)
MESH = pl.DeviceIdType.MESH


def merge(parts, stats):
    top = functools.reduce(jnp.maximum, stats)
    shares = [jnp.exp(stat - top) for stat in stats]
    total = functools.reduce(jnp.add, shares)
    scale = 1.0 / total
    merged = functools.reduce(
        jnp.add, [part * (share * scale) for part, share in zip(parts, shares)]
    )
    return merged, top + jnp.log(total)


def far_first(n):
    return sorted(range(1, n), key=lambda step: -min(step, n - step))


def merge_slots(slots, stats):
    n = slots.shape[0]
    return merge(
        [slots[j].astype(jnp.float32) for j in range(n)], [stats[j] for j in range(n)]
    )


def kernel(
    nk, n,
    len_hbm, q_hbm, k_hbm, v_hbm, w_hbm, out_ref,
    len_ref, q_ref, k_ref, v_ref, w_ref, vt_ref, wt_ref, scores,
    send1, recv1, recv2, stat0, stat1, stat2, att, send3, recv3,
    load_sem, send_sem, recv_sem,
):
    rows = q_ref.shape[0]
    keys = k_ref.shape[0]
    pairs = n // 2
    kvh = lax.axis_index("kvh")
    ctx = lax.axis_index("ctx")
    y, z = ctx // n, lax.rem(ctx, n)
    mine = (y, z)

    load_k = pltpu.make_async_copy(k_hbm, k_ref.at[:, pl.ds(0, HD)], load_sem.at[0])
    load_q = pltpu.make_async_copy(q_hbm, q_ref, load_sem.at[1])
    load_len = pltpu.make_async_copy(len_hbm, len_ref, load_sem.at[2])
    load_v = pltpu.make_async_copy(v_hbm, v_ref, load_sem.at[3])
    load_w = pltpu.make_async_copy(w_hbm, w_ref, load_sem.at[4])
    load_k.start()
    load_q.start()
    load_len.start()

    def along(kind, to):
        return (kvh, to * n + z) if kind == 0 else (kvh, y * n + to)

    def on_kvh(step):
        return (lax.rem(kvh + step, nk), ctx)

    barrier = pltpu.get_barrier_semaphore()
    for step in far_first(n):
        for kind in range(2):
            device = along(kind, lax.rem(mine[kind] + step, n))
            pl.semaphore_signal(barrier, inc=1, device_id=device, device_id_type=MESH)
    for step in range(1, nk):
        pl.semaphore_signal(barrier, inc=1, device_id=on_kvh(step), device_id_type=MESH)

    load_v.start()
    load_w.start()

    def send(src, dst, index, device):
        pltpu.make_async_remote_copy(
            src_ref=src, dst_ref=dst, send_sem=send_sem.at[index],
            recv_sem=recv_sem.at[index], device_id=device, device_id_type=MESH,
        ).start()

    def take(ref, sem):
        pltpu.make_async_copy(ref, ref, sem).wait()

    lane = lax.broadcasted_iota(jnp.int32, (2 * rows, HD), 1)
    unit = jnp.where(lane == 0, 1.0, 0.0).astype(jnp.bfloat16)
    position = lax.broadcasted_iota(jnp.int32, (keys, HD), 0)
    column = lax.broadcasted_iota(jnp.int32, (keys, HD), 1)
    load_len.wait()
    bias = jnp.where((column == 0) & (position >= len_ref[0]), MASKED, 0.0)
    k_ref[:, HD:] = bias.astype(jnp.bfloat16)

    orders = [
        [lax.rem(mine[kind] // 2 + step, pairs) for step in far_first(pairs) + [0]]
        for kind in range(2)
    ]

    def give(kind, place, owner):
        device = along(kind, owner)
        send(send1.at[kind, owner], recv1.at[kind, mine[kind]], kind, device)
        send(stat0.at[kind, place], stat1.at[kind, mine[kind]], 7 + kind, device)

    def score(pair):
        heads = [orders[kind][pair] + kind * pairs for kind in range(2)]
        query = jnp.concatenate(
            [q_ref[:, pl.ds(pl.multiple_of(h * HD, HD), HD)] for h in heads], axis=0
        )
        query = jnp.concatenate([query, unit], axis=1)
        scores[pair % 2] = lax.dot_general(
            k_ref[...], query, (((1,), (1,)), ((), ())),
            preferred_element_type=jnp.float32,
        )

    load_q.wait()
    load_k.wait()
    score(0)
    load_v.wait()
    vt_ref[:HD] = v_ref[...].T
    vt_ref[HD:] = jnp.ones((ONE_ROWS, keys), jnp.bfloat16)
    for pair in range(pairs):
        if pair + 1 < pairs:
            score(pair + 1)
        block = scores[pair % 2]
        peak = jnp.max(block, axis=0, keepdims=True)
        weights = jnp.exp2((block - peak) * (SCALE * LOG2E)).astype(jnp.bfloat16)
        outs = jnp.dot(vt_ref[...], weights, preferred_element_type=jnp.float32)
        total = outs[HD : HD + 1]
        stat = peak * SCALE + jnp.log(total)
        outs = (outs[:HD] * (1.0 / total)).astype(jnp.bfloat16)
        if pair == 0:
            pl.semaphore_wait(barrier, 2 * (n - 1) + nk - 1)
        for kind in range(2):
            here = slice(kind * rows, (kind + 1) * rows)
            place = orders[kind][pair]
            stat0[kind, place] = stat[:, here]
            for half in range(2):
                owner = place * 2 + half
                send1[kind, owner] = outs[half * HALF : (half + 1) * HALF, here]
                if pair + 1 < pairs:
                    give(kind, place, owner)
            if pair + 1 == pairs:
                own = mine[kind]
                give(kind, place, own + 1 - 2 * lax.rem(own, 2))
                recv1[kind, own] = send1[kind, own]
                stat1[kind, own] = stat[:, here]

    load_w.wait()
    wt_ref[...] = w_ref[...].T

    for kind in range(2):
        take(recv1.at[kind, pl.ds(0, n - 1)], recv_sem.at[kind])
        take(stat1.at[kind, pl.ds(0, n - 1)], recv_sem.at[7 + kind])
        merged, stat = merge_slots(recv1.at[kind], stat1.at[kind])
        across = mine[1 - kind]
        slot = recv2.at[kind, across]
        slot[...] = merged.astype(jnp.bfloat16)
        stat2[kind, across] = stat
        for step in far_first(n):
            to = lax.rem(across + step, n)
            send(slot, slot, 2 + kind, along(1 - kind, to))
            row = stat2.at[kind, across]
            send(row, row, 9 + kind, along(1 - kind, to))

    for kind in range(2):
        take(recv2.at[kind, pl.ds(0, n - 1)], recv_sem.at[2 + kind])
        take(stat2.at[kind, pl.ds(0, n - 1)], recv_sem.at[9 + kind])
        merged, _ = merge_slots(recv2.at[kind], stat2.at[kind])
        slot = att.at[kind, mine[kind]]
        slot[...] = merged.astype(jnp.bfloat16)
        for step in far_first(n):
            to = lax.rem(mine[kind] + step, n)
            send(slot, slot, 4 + kind, along(kind, to))

    mixed = None
    for kind in range(2):
        take(att.at[kind, pl.ds(0, n - 1)], recv_sem.at[4 + kind])
        part = jnp.dot(
            wt_ref[:, kind * n * HALF : (kind + 1) * n * HALF],
            att[kind].reshape(n * HALF, rows),
            preferred_element_type=jnp.float32,
        )
        mixed = part if mixed is None else mixed + part
    send3[...] = mixed.T.reshape(send3.shape)
    for step in far_first(nk):
        to = lax.rem(kvh + step, nk)
        send(send3.at[to], recv3.at[kvh], 6, on_kvh(step))
    recv3[kvh] = send3[kvh]
    take(recv3.at[pl.ds(0, nk - 1)], recv_sem.at[6])
    out_ref[...] = jnp.sum(recv3[...], axis=0).astype(jnp.bfloat16)

    for kind in range(2):
        take(send1.at[kind, pl.ds(0, n - 1)], send_sem.at[kind])
        take(stat1.at[kind, pl.ds(0, n - 1)], send_sem.at[7 + kind])
        take(recv2.at[kind, pl.ds(0, n - 1)], send_sem.at[2 + kind])
        take(stat2.at[kind, pl.ds(0, n - 1)], send_sem.at[9 + kind])
        take(att.at[kind, pl.ds(0, n - 1)], send_sem.at[4 + kind])
    take(send3.at[pl.ds(0, nk - 1)], send_sem.at[6])


def solution(mesh):
    nk = mesh.shape["kvh"]
    n = math.isqrt(mesh.shape["ctx"])

    def step(queries, cache_keys, cache_values, lengths, w_out):
        rows, keys = queries.shape[0], cache_keys.shape[0]
        bf16, f32 = jnp.bfloat16, jnp.float32
        in_hbm = pl.BlockSpec(memory_space=pltpu.HBM)
        return pl.pallas_call(
            functools.partial(kernel, nk, n),
            out_shape=jax.ShapeDtypeStruct((rows // nk, HD), bf16),
            in_specs=[in_hbm] * 5,
            out_specs=pl.BlockSpec(memory_space=pltpu.VMEM),
            scratch_shapes=[
                pltpu.SMEM((1,), jnp.int32),
                pltpu.VMEM(queries.shape, bf16),
                pltpu.VMEM((keys, 2 * HD), bf16),
                pltpu.VMEM((keys, HD), bf16),
                pltpu.VMEM(w_out.shape, bf16),
                pltpu.VMEM((HD + ONE_ROWS, keys), bf16),
                pltpu.VMEM((HD, n * HD), bf16),
                pltpu.VMEM((2, keys, 2 * rows), f32),
                pltpu.VMEM((2, n, HALF, rows), bf16),
                pltpu.VMEM((2, n, HALF, rows), bf16),
                pltpu.VMEM((2, n, HALF, rows), bf16),
                pltpu.VMEM((2, n // 2, 1, rows), f32),
                pltpu.VMEM((2, n, 1, rows), f32),
                pltpu.VMEM((2, n, 1, rows), f32),
                pltpu.VMEM((2, n, HALF, rows), bf16),
                pltpu.VMEM((nk, rows // nk, HD), f32),
                pltpu.VMEM((nk, rows // nk, HD), f32),
                pltpu.SemaphoreType.DMA((5,)),
                pltpu.SemaphoreType.DMA((11,)),
                pltpu.SemaphoreType.DMA((11,)),
            ],
            compiler_params=pltpu.CompilerParams(
                collective_id=0, has_side_effects=True, vmem_limit_bytes=VMEM_BYTES
            ),
        )(lengths, queries, cache_keys, cache_values, w_out)

    in_specs = (P(None, "kvh"), P("ctx", "kvh"), P("ctx", "kvh"), P("ctx"), P("kvh", "ctx"))
    out_specs = P("kvh", "ctx")
    return jax.shard_map(step, mesh=mesh, in_specs=in_specs, out_specs=out_specs, check_vma=False)
```

```python
import functools
import math

import jax
import jax.numpy as jnp
from jax import lax
from jax.experimental import pallas as pl
from jax.experimental.pallas import tpu as pltpu
from jax.sharding import PartitionSpec as P

HD = 128
HALF = HD // 2
ONE_ROWS = 16
VMEM_BYTES = 53 * 2**20 + 800 * 2**10
MASKED = -1e30
SCALE = 1.0 / math.sqrt(HD)
LOG2E = math.log2(math.e)
MESH = pl.DeviceIdType.MESH


def shares_of(stats):
    rows = [stats[j] for j in range(stats.shape[0])]
    top = functools.reduce(jnp.maximum, rows)
    shares = [jnp.exp(row - top) for row in rows]
    total = functools.reduce(jnp.add, shares)
    scale = 1.0 / total
    return [share * scale for share in shares], top + jnp.log(total)


def merge(slots, shares):
    return functools.reduce(
        jnp.add,
        [slots[j].astype(jnp.float32) * share for j, share in enumerate(shares)],
    ).astype(jnp.bfloat16)


def far_first(n):
    return sorted(range(1, n), key=lambda step: -min(step, n - step))


def kernel(
    nk, n,
    len_ref, q_hbm, k_hbm, v_hbm, w_hbm, out_ref,
    q_ref, k_ref, v_ref, w_ref, vt_ref, wt_ref, scores,
    send1, recv1, recv2, stat0, stat1, stat2, att, send3, recv3,
    load_sem, send_sem, recv_sem,
):
    rows = q_ref.shape[0]
    keys = k_ref.shape[0]
    pairs = n // 2
    kvh = lax.axis_index("kvh")
    ctx = lax.axis_index("ctx")
    y, z = ctx // n, lax.rem(ctx, n)
    mine = (y, z)

    load_k = pltpu.make_async_copy(k_hbm, k_ref.at[:, pl.ds(0, HD)], load_sem.at[0])
    load_q = pltpu.make_async_copy(q_hbm, q_ref, load_sem.at[1])
    load_v = pltpu.make_async_copy(v_hbm, v_ref, load_sem.at[2])
    load_w = pltpu.make_async_copy(w_hbm, w_ref, load_sem.at[3])
    load_k.start()
    load_q.start()

    def along(kind, to):
        return (kvh, to * n + z) if kind == 0 else (kvh, y * n + to)

    def on_kvh(step):
        return (lax.rem(kvh + step, nk), ctx)

    barrier = pltpu.get_barrier_semaphore()
    for step in far_first(n):
        for kind in range(2):
            device = along(kind, lax.rem(mine[kind] + step, n))
            pl.semaphore_signal(barrier, inc=1, device_id=device, device_id_type=MESH)
    for step in range(1, nk):
        pl.semaphore_signal(barrier, inc=1, device_id=on_kvh(step), device_id_type=MESH)

    load_v.start()
    load_w.start()

    def send(src, dst, index, device):
        pltpu.make_async_remote_copy(
            src_ref=src, dst_ref=dst, send_sem=send_sem.at[index],
            recv_sem=recv_sem.at[index], device_id=device, device_id_type=MESH,
        ).start()

    def take(ref, sem):
        pltpu.make_async_copy(ref, ref, sem).wait()

    lane = lax.broadcasted_iota(jnp.int32, (2 * rows, HD), 1)
    unit = jnp.where(lane == 0, 1.0, 0.0).astype(jnp.bfloat16)
    position = lax.broadcasted_iota(jnp.int32, (keys, HD), 0)
    column = lax.broadcasted_iota(jnp.int32, (keys, HD), 1)
    bias = jnp.where((column == 0) & (position >= len_ref[0]), MASKED, 0.0)
    k_ref[:, HD:] = bias.astype(jnp.bfloat16)

    orders = [
        [lax.rem(mine[kind] // 2 + step, pairs) for step in far_first(pairs) + [0]]
        for kind in range(2)
    ]

    def give(kind, place, owner):
        device = along(kind, owner)
        send(stat0.at[kind, place], stat1.at[kind, mine[kind]], 7 + kind, device)
        send(send1.at[kind, owner], recv1.at[kind, mine[kind]], kind, device)

    def score(pair):
        heads = [orders[kind][pair] + kind * pairs for kind in range(2)]
        query = jnp.concatenate(
            [q_ref[:, pl.ds(pl.multiple_of(h * HD, HD), HD)] for h in heads], axis=0
        )
        query = jnp.concatenate([query, unit], axis=1)
        scores[pair % 2] = lax.dot_general(
            k_ref[...], query, (((1,), (1,)), ((), ())),
            preferred_element_type=jnp.float32,
        )

    load_q.wait()
    load_k.wait()
    score(0)
    load_v.wait()
    vt_ref[:HD] = v_ref[...].T
    vt_ref[HD:] = jnp.ones((ONE_ROWS, keys), jnp.bfloat16)
    for pair in range(pairs):
        if pair + 1 < pairs:
            score(pair + 1)
        block = scores[pair % 2]
        peak = jnp.max(block, axis=0, keepdims=True)
        weights = jnp.exp2((block - peak) * (SCALE * LOG2E)).astype(jnp.bfloat16)
        outs = jnp.dot(vt_ref[...], weights, preferred_element_type=jnp.float32)
        total = outs[HD : HD + 1]
        stat = peak * SCALE + jnp.log(total)
        outs = (outs[:HD] * (1.0 / total)).astype(jnp.bfloat16)
        if pair == 0:
            pl.semaphore_wait(barrier, 2 * (n - 1) + nk - 1)
        for kind in range(2):
            here = slice(kind * rows, (kind + 1) * rows)
            place = orders[kind][pair]
            stat0[kind, place] = stat[:, here]
            for half in range(2):
                owner = place * 2 + half
                send1[kind, owner] = outs[half * HALF : (half + 1) * HALF, here]
                if pair + 1 < pairs:
                    give(kind, place, owner)
            if pair + 1 == pairs:
                own = mine[kind]
                give(kind, place, own + 1 - 2 * lax.rem(own, 2))
                recv1[kind, own] = send1[kind, own]
                stat1[kind, own] = stat[:, here]

    load_w.wait()
    wt_ref[...] = w_ref[...].T

    for kind in range(2):
        take(stat1.at[kind, pl.ds(0, n - 1)], recv_sem.at[7 + kind])
        shares, stat = shares_of(stat1.at[kind])
        across = mine[1 - kind]
        row, slot = stat2.at[kind, across], recv2.at[kind, across]
        row[...] = stat
        take(recv1.at[kind, pl.ds(0, n - 1)], recv_sem.at[kind])
        slot[...] = merge(recv1.at[kind], shares)
        for step in far_first(n):
            device = along(1 - kind, lax.rem(across + step, n))
            send(row, row, 9 + kind, device)
            send(slot, slot, 2 + kind, device)

    for kind in range(2):
        take(stat2.at[kind, pl.ds(0, n - 1)], recv_sem.at[9 + kind])
        shares, _ = shares_of(stat2.at[kind])
        slot = att.at[kind, mine[kind]]
        take(recv2.at[kind, pl.ds(0, n - 1)], recv_sem.at[2 + kind])
        slot[...] = merge(recv2.at[kind], shares)
        for step in far_first(n):
            device = along(kind, lax.rem(mine[kind] + step, n))
            send(slot, slot, 4 + kind, device)

    mixed = None
    for kind in range(2):
        take(att.at[kind, pl.ds(0, n - 1)], recv_sem.at[4 + kind])
        part = jnp.dot(
            wt_ref[:, kind * n * HALF : (kind + 1) * n * HALF],
            att[kind].reshape(n * HALF, rows),
            preferred_element_type=jnp.float32,
        )
        mixed = part if mixed is None else mixed + part
    send3[...] = mixed.T.reshape(send3.shape)
    for step in far_first(nk):
        to = lax.rem(kvh + step, nk)
        send(send3.at[to], recv3.at[kvh], 6, on_kvh(step))
    recv3[kvh] = send3[kvh]

    for kind in range(2):
        take(send1.at[kind, pl.ds(0, n - 1)], send_sem.at[kind])
        take(stat1.at[kind, pl.ds(0, n - 1)], send_sem.at[7 + kind])
        take(recv2.at[kind, pl.ds(0, n - 1)], send_sem.at[2 + kind])
        take(stat2.at[kind, pl.ds(0, n - 1)], send_sem.at[9 + kind])
        take(att.at[kind, pl.ds(0, n - 1)], send_sem.at[4 + kind])

    take(recv3.at[pl.ds(0, nk - 1)], recv_sem.at[6])
    out_ref[...] = jnp.sum(recv3[...], axis=0).astype(jnp.bfloat16)
    take(send3.at[pl.ds(0, nk - 1)], send_sem.at[6])


def solution(mesh):
    nk = mesh.shape["kvh"]
    n = math.isqrt(mesh.shape["ctx"])

    def step(queries, cache_keys, cache_values, lengths, w_out):
        rows, keys = queries.shape[0], cache_keys.shape[0]
        bf16, f32 = jnp.bfloat16, jnp.float32
        in_hbm = pl.BlockSpec(memory_space=pltpu.HBM)
        return pl.pallas_call(
            functools.partial(kernel, nk, n),
            out_shape=jax.ShapeDtypeStruct((rows // nk, HD), bf16),
            in_specs=[pl.BlockSpec(memory_space=pltpu.SMEM)] + [in_hbm] * 4,
            out_specs=pl.BlockSpec(memory_space=pltpu.VMEM),
            scratch_shapes=[
                pltpu.VMEM(queries.shape, bf16),
                pltpu.VMEM((keys, 2 * HD), bf16),
                pltpu.VMEM((keys, HD), bf16),
                pltpu.VMEM(w_out.shape, bf16),
                pltpu.VMEM((HD + ONE_ROWS, keys), bf16),
                pltpu.VMEM((HD, n * HD), bf16),
                pltpu.VMEM((2, keys, 2 * rows), f32),
                pltpu.VMEM((2, n, HALF, rows), bf16),
                pltpu.VMEM((2, n, HALF, rows), bf16),
                pltpu.VMEM((2, n, HALF, rows), bf16),
                pltpu.VMEM((2, n // 2, 1, rows), f32),
                pltpu.VMEM((2, n, 1, rows), f32),
                pltpu.VMEM((2, n, 1, rows), f32),
                pltpu.VMEM((2, n, HALF, rows), bf16),
                pltpu.VMEM((nk, rows // nk, HD), f32),
                pltpu.VMEM((nk, rows // nk, HD), f32),
                pltpu.SemaphoreType.DMA((4,)),
                pltpu.SemaphoreType.DMA((11,)),
                pltpu.SemaphoreType.DMA((11,)),
            ],
            compiler_params=pltpu.CompilerParams(
                collective_id=0, has_side_effects=True, vmem_limit_bytes=VMEM_BYTES
            ),
        )(lengths, queries, cache_keys, cache_values, w_out)

    in_specs = (P(None, "kvh"), P("ctx", "kvh"), P("ctx", "kvh"), P("ctx"), P("kvh", "ctx"))
    out_specs = P("kvh", "ctx")
    return jax.shard_map(step, mesh=mesh, in_specs=in_specs, out_specs=out_specs, check_vma=False)
```

```python
import functools
import math

import jax
import jax.numpy as jnp
from jax import lax
from jax.experimental import pallas as pl
from jax.experimental.pallas import tpu as pltpu
from jax.sharding import PartitionSpec as P

HD = 128
HALF = HD // 2
ONE_ROWS = 16
VMEM_BYTES = 53 * 2**20 + 800 * 2**10
MASKED = -1e30
SCALE = 1.0 / math.sqrt(HD)
LOG2E = math.log2(math.e)
MESH = pl.DeviceIdType.MESH


def shares_of(stats):
    rows = [stats[j] for j in range(stats.shape[0])]
    top = functools.reduce(jnp.maximum, rows)
    shares = [jnp.exp(row - top) for row in rows]
    total = functools.reduce(jnp.add, shares)
    scale = 1.0 / total
    return [share * scale for share in shares], top + jnp.log(total)


def merge(slots, shares):
    return functools.reduce(
        jnp.add,
        [slots[j].astype(jnp.float32) * share for j, share in enumerate(shares)],
    ).astype(jnp.bfloat16)


def far_first(n):
    return sorted(range(1, n), key=lambda step: -min(step, n - step))


def kernel(
    nk, n,
    len_ref, q_hbm, k_hbm, v_hbm, w_hbm, out_ref,
    q_ref, k_ref, v_ref, w_ref, vt_ref, wt_ref, scores,
    send1, recv1, recv2, stat0, stat1, stat2, att, send3, recv3,
    load_sem, send_sem, recv_sem,
):
    rows = q_ref.shape[0]
    keys = k_ref.shape[0]
    pairs = n // 2
    kvh = lax.axis_index("kvh")
    ctx = lax.axis_index("ctx")
    y, z = ctx // n, lax.rem(ctx, n)
    mine = (y, z)

    load_k = pltpu.make_async_copy(k_hbm, k_ref.at[:, pl.ds(0, HD)], load_sem.at[0])
    load_q = pltpu.make_async_copy(q_hbm, q_ref, load_sem.at[1])
    load_v = pltpu.make_async_copy(v_hbm, v_ref, load_sem.at[2])
    load_w = pltpu.make_async_copy(w_hbm, w_ref, load_sem.at[3])
    load_k.start()
    load_q.start()
    load_v.start()
    load_w.start()

    def along(kind, to):
        return (kvh, to * n + z) if kind == 0 else (kvh, y * n + to)

    def on_kvh(step):
        return (lax.rem(kvh + step, nk), ctx)

    barrier = pltpu.get_barrier_semaphore()
    for step in far_first(n):
        for kind in range(2):
            device = along(kind, lax.rem(mine[kind] + step, n))
            pl.semaphore_signal(barrier, inc=1, device_id=device, device_id_type=MESH)
    for step in range(1, nk):
        pl.semaphore_signal(barrier, inc=1, device_id=on_kvh(step), device_id_type=MESH)

    def send(src, dst, index, device):
        pltpu.make_async_remote_copy(
            src_ref=src, dst_ref=dst, send_sem=send_sem.at[index],
            recv_sem=recv_sem.at[index], device_id=device, device_id_type=MESH,
        ).start()

    def take(ref, sem):
        pltpu.make_async_copy(ref, ref, sem).wait()

    lane = lax.broadcasted_iota(jnp.int32, (2 * rows, HD), 1)
    unit = jnp.where(lane == 0, 1.0, 0.0).astype(jnp.bfloat16)
    position = lax.broadcasted_iota(jnp.int32, (keys, HD), 0)
    column = lax.broadcasted_iota(jnp.int32, (keys, HD), 1)
    bias = jnp.where((column == 0) & (position >= len_ref[0]), MASKED, 0.0)
    k_ref[:, HD:] = bias.astype(jnp.bfloat16)

    orders = []
    for kind in range(2):
        place, odd = mine[kind] // 2, lax.rem(mine[kind], 2)
        steps = far_first(pairs) + [0]
        if pairs == 4:
            steps = [2, 1 + 2 * odd, 3 - 2 * odd, 0]
        orders.append([lax.rem(place + step, pairs) for step in steps])

    def give(kind, place, owner):
        device = along(kind, owner)
        send(stat0.at[kind, place], stat1.at[kind, mine[kind]], 7 + kind, device)
        send(send1.at[kind, owner], recv1.at[kind, mine[kind]], kind, device)

    def score(pair):
        heads = [orders[kind][pair] + kind * pairs for kind in range(2)]
        query = jnp.concatenate(
            [q_ref[:, pl.ds(pl.multiple_of(h * HD, HD), HD)] for h in heads], axis=0
        )
        query = jnp.concatenate([query, unit], axis=1)
        scores[pair % 2] = lax.dot_general(
            k_ref[...], query, (((1,), (1,)), ((), ())),
            preferred_element_type=jnp.float32,
        )

    load_q.wait()
    load_k.wait()
    score(0)
    load_v.wait()
    vt_ref[:HD] = v_ref[...].T
    vt_ref[HD:] = jnp.ones((ONE_ROWS, keys), jnp.bfloat16)
    for pair in range(pairs):
        if pair + 1 < pairs:
            score(pair + 1)
        block = scores[pair % 2]
        peak = jnp.max(block, axis=0, keepdims=True)
        weights = jnp.exp2((block - peak) * (SCALE * LOG2E)).astype(jnp.bfloat16)
        outs = jnp.dot(vt_ref[...], weights, preferred_element_type=jnp.float32)
        total = outs[HD : HD + 1]
        stat = peak * SCALE + jnp.log(total)
        outs = (outs[:HD] * (1.0 / total)).astype(jnp.bfloat16)
        if pair == 0:
            pl.semaphore_wait(barrier, 2 * (n - 1) + nk - 1)
        for kind in range(2):
            here = slice(kind * rows, (kind + 1) * rows)
            place = orders[kind][pair]
            stat0[kind, place] = stat[:, here]
            for half in range(2):
                owner = place * 2 + half
                send1[kind, owner] = outs[half * HALF : (half + 1) * HALF, here]
                if pair + 1 < pairs:
                    give(kind, place, owner)
            if pair + 1 == pairs:
                own = mine[kind]
                give(kind, place, own + 1 - 2 * lax.rem(own, 2))
                recv1[kind, own] = send1[kind, own]
                stat1[kind, own] = stat[:, here]

    load_w.wait()
    wt_ref[...] = w_ref[...].T

    for kind in range(2):
        take(stat1.at[kind, pl.ds(0, n - 1)], recv_sem.at[7 + kind])
        shares, stat = shares_of(stat1.at[kind])
        across = mine[1 - kind]
        row, slot = stat2.at[kind, across], recv2.at[kind, across]
        row[...] = stat
        take(recv1.at[kind, pl.ds(0, n - 1)], recv_sem.at[kind])
        slot[...] = merge(recv1.at[kind], shares)
        for step in far_first(n):
            device = along(1 - kind, lax.rem(across + step, n))
            send(row, row, 9 + kind, device)
            send(slot, slot, 2 + kind, device)

    for kind in range(2):
        take(stat2.at[kind, pl.ds(0, n - 1)], recv_sem.at[9 + kind])
        shares, _ = shares_of(stat2.at[kind])
        slot = att.at[kind, mine[kind]]
        take(recv2.at[kind, pl.ds(0, n - 1)], recv_sem.at[2 + kind])
        slot[...] = merge(recv2.at[kind], shares)
        for step in far_first(n):
            device = along(kind, lax.rem(mine[kind] + step, n))
            send(slot, slot, 4 + kind, device)

    mixed = None
    for kind in range(2):
        take(att.at[kind, pl.ds(0, n - 1)], recv_sem.at[4 + kind])
        part = jnp.dot(
            wt_ref[:, kind * n * HALF : (kind + 1) * n * HALF],
            att[kind].reshape(n * HALF, rows),
            preferred_element_type=jnp.float32,
        )
        mixed = part if mixed is None else mixed + part
    send3[...] = mixed.T.reshape(send3.shape)
    for step in far_first(nk):
        to = lax.rem(kvh + step, nk)
        send(send3.at[to], recv3.at[kvh], 6, on_kvh(step))
    recv3[kvh] = send3[kvh]

    for kind in range(2):
        take(send1.at[kind, pl.ds(0, n - 1)], send_sem.at[kind])
        take(stat1.at[kind, pl.ds(0, n - 1)], send_sem.at[7 + kind])
        take(recv2.at[kind, pl.ds(0, n - 1)], send_sem.at[2 + kind])
        take(stat2.at[kind, pl.ds(0, n - 1)], send_sem.at[9 + kind])
        take(att.at[kind, pl.ds(0, n - 1)], send_sem.at[4 + kind])

    take(recv3.at[pl.ds(0, nk - 1)], recv_sem.at[6])
    out_ref[...] = jnp.sum(recv3[...], axis=0).astype(jnp.bfloat16)
    take(send3.at[pl.ds(0, nk - 1)], send_sem.at[6])


def solution(mesh):
    nk = mesh.shape["kvh"]
    n = math.isqrt(mesh.shape["ctx"])

    def step(queries, cache_keys, cache_values, lengths, w_out):
        rows, keys = queries.shape[0], cache_keys.shape[0]
        bf16, f32 = jnp.bfloat16, jnp.float32
        in_hbm = pl.BlockSpec(memory_space=pltpu.HBM)
        return pl.pallas_call(
            functools.partial(kernel, nk, n),
            out_shape=jax.ShapeDtypeStruct((rows // nk, HD), bf16),
            in_specs=[pl.BlockSpec(memory_space=pltpu.SMEM)] + [in_hbm] * 4,
            out_specs=pl.BlockSpec(memory_space=pltpu.VMEM),
            scratch_shapes=[
                pltpu.VMEM(queries.shape, bf16),
                pltpu.VMEM((keys, 2 * HD), bf16),
                pltpu.VMEM((keys, HD), bf16),
                pltpu.VMEM(w_out.shape, bf16),
                pltpu.VMEM((HD + ONE_ROWS, keys), bf16),
                pltpu.VMEM((HD, n * HD), bf16),
                pltpu.VMEM((2, keys, 2 * rows), f32),
                pltpu.VMEM((2, n, HALF, rows), bf16),
                pltpu.VMEM((2, n, HALF, rows), bf16),
                pltpu.VMEM((2, n, HALF, rows), bf16),
                pltpu.VMEM((2, n // 2, 1, rows), f32),
                pltpu.VMEM((2, n, 1, rows), f32),
                pltpu.VMEM((2, n, 1, rows), f32),
                pltpu.VMEM((2, n, HALF, rows), bf16),
                pltpu.VMEM((nk, rows // nk, HD), f32),
                pltpu.VMEM((nk, rows // nk, HD), f32),
                pltpu.SemaphoreType.DMA((4,)),
                pltpu.SemaphoreType.DMA((11,)),
                pltpu.SemaphoreType.DMA((11,)),
            ],
            compiler_params=pltpu.CompilerParams(
                collective_id=0, has_side_effects=True, vmem_limit_bytes=VMEM_BYTES
            ),
        )(lengths, queries, cache_keys, cache_values, w_out)

    in_specs = (P(None, "kvh"), P("ctx", "kvh"), P("ctx", "kvh"), P("ctx"), P("kvh", "ctx"))
    out_specs = P("kvh", "ctx")
    return jax.shard_map(step, mesh=mesh, in_specs=in_specs, out_specs=out_specs, check_vma=False)
```

```python
import functools
import math

import jax
import jax.numpy as jnp
from jax import lax
from jax.experimental import pallas as pl
from jax.experimental.pallas import tpu as pltpu
from jax.sharding import PartitionSpec as P

HD = 128
HALF = HD // 2
ONE_ROWS = 16
VMEM_BYTES = 53 * 2**20 + 800 * 2**10
MASKED = -1e30
SCALE = 1.0 / math.sqrt(HD)
LOG2E = math.log2(math.e)
MESH = pl.DeviceIdType.MESH


def shares_of(stats):
    rows = [stats[j] for j in range(stats.shape[0])]
    top = functools.reduce(jnp.maximum, rows)
    shares = [jnp.exp(row - top) for row in rows]
    total = functools.reduce(jnp.add, shares)
    scale = 1.0 / total
    return [share * scale for share in shares], top + jnp.log(total)


def merge(slots, shares):
    return functools.reduce(
        jnp.add,
        [slots[j].astype(jnp.float32) * share for j, share in enumerate(shares)],
    ).astype(jnp.bfloat16)


def far_first(n):
    return sorted(range(1, n), key=lambda step: -min(step, n - step))


def kernel(
    nk, n,
    len_ref, q_hbm, k_hbm, v_hbm, w_hbm, out_ref,
    q_ref, k_ref, v_ref, w_ref, vt_ref, wt_ref, scores,
    send1, recv1, recv2, stat0, stat1, stat2, att, send3, recv3,
    load_sem, send_sem, recv_sem,
):
    rows = q_ref.shape[0]
    keys = k_ref.shape[0]
    pairs = n // 2
    kvh = lax.axis_index("kvh")
    ctx = lax.axis_index("ctx")
    y, z = ctx // n, lax.rem(ctx, n)
    mine = (y, z)

    load_k = pltpu.make_async_copy(k_hbm, k_ref.at[:, pl.ds(0, HD)], load_sem.at[0])
    load_q = pltpu.make_async_copy(q_hbm, q_ref, load_sem.at[1])
    load_v = pltpu.make_async_copy(v_hbm, v_ref, load_sem.at[2])
    load_w = pltpu.make_async_copy(w_hbm, w_ref, load_sem.at[3])
    load_k.start()
    load_q.start()
    load_v.start()
    load_w.start()

    def along(kind, to):
        return (kvh, to * n + z) if kind == 0 else (kvh, y * n + to)

    def on_kvh(step):
        return (lax.rem(kvh + step, nk), ctx)

    barrier = pltpu.get_barrier_semaphore()
    for step in far_first(n):
        for kind in range(2):
            device = along(kind, lax.rem(mine[kind] + step, n))
            pl.semaphore_signal(barrier, inc=1, device_id=device, device_id_type=MESH)
    for step in range(1, nk):
        pl.semaphore_signal(barrier, inc=1, device_id=on_kvh(step), device_id_type=MESH)

    def send(src, dst, index, device):
        pltpu.make_async_remote_copy(
            src_ref=src, dst_ref=dst, send_sem=send_sem.at[index],
            recv_sem=recv_sem.at[index], device_id=device, device_id_type=MESH,
        ).start()

    def take(ref, sem):
        pltpu.make_async_copy(ref, ref, sem).wait()

    lane = lax.broadcasted_iota(jnp.int32, (2 * rows, HD), 1)
    unit = jnp.where(lane == 0, 1.0, 0.0).astype(jnp.bfloat16)
    position = lax.broadcasted_iota(jnp.int32, (keys, HD), 0)
    column = lax.broadcasted_iota(jnp.int32, (keys, HD), 1)
    bias = jnp.where((column == 0) & (position >= len_ref[0]), MASKED, 0.0)
    k_ref[:, HD:] = bias.astype(jnp.bfloat16)

    orders = []
    for kind in range(2):
        place, odd = mine[kind] // 2, lax.rem(mine[kind], 2)
        steps = far_first(pairs) + [0]
        if pairs == 4:
            steps = [2, 1 + 2 * odd, 3 - 2 * odd, 0]
        orders.append([lax.rem(place + step, pairs) for step in steps])

    def give(kind, place, owner):
        device = along(kind, owner)
        send(stat0.at[kind, place], stat1.at[kind, mine[kind]], 7 + kind, device)
        send(send1.at[kind, owner], recv1.at[kind, mine[kind]], kind, device)

    def score(pair):
        heads = [orders[kind][pair] + kind * pairs for kind in range(2)]
        query = jnp.concatenate(
            [q_ref[:, pl.ds(pl.multiple_of(h * HD, HD), HD)] for h in heads], axis=0
        )
        query = jnp.concatenate([query, unit], axis=1)
        scores[pair % 2] = lax.dot_general(
            k_ref[...], query, (((1,), (1,)), ((), ())),
            preferred_element_type=jnp.float32,
        )

    load_q.wait()
    load_k.wait()
    score(0)
    load_v.wait()
    vt_ref[:HD] = v_ref[...].T
    vt_ref[HD:] = jnp.ones((ONE_ROWS, keys), jnp.bfloat16)
    for pair in range(pairs):
        if pair + 1 < pairs:
            score(pair + 1)
        block = scores[pair % 2]
        peak = jnp.max(block, axis=0, keepdims=True)
        weights = jnp.exp2((block - peak) * (SCALE * LOG2E)).astype(jnp.bfloat16)
        outs = jnp.dot(vt_ref[...], weights, preferred_element_type=jnp.float32)
        total = outs[HD : HD + 1]
        stat = peak * SCALE + jnp.log(total)
        outs = (outs[:HD] * (1.0 / total)).astype(jnp.bfloat16)
        if pair == 0:
            pl.semaphore_wait(barrier, 2 * (n - 1) + nk - 1)
        for kind in range(2):
            here = slice(kind * rows, (kind + 1) * rows)
            place = orders[kind][pair]
            stat0[kind, place] = stat[:, here]
            for half in range(2):
                owner = place * 2 + half
                send1[kind, owner] = outs[half * HALF : (half + 1) * HALF, here]
                if pair + 1 < pairs:
                    give(kind, place, owner)
            if pair + 1 == pairs:
                own = mine[kind]
                give(kind, place, own + 1 - 2 * lax.rem(own, 2))
                recv1[kind, own] = send1[kind, own]
                stat1[kind, own] = stat[:, here]

    load_w.wait()
    wt_ref[...] = w_ref[...].T

    for kind in range(2):
        take(stat1.at[kind, pl.ds(0, n - 1)], recv_sem.at[7 + kind])
        shares, stat = shares_of(stat1.at[kind])
        across = mine[1 - kind]
        row, slot = stat2.at[kind, across], recv2.at[kind, across]
        row[...] = stat
        take(recv1.at[kind, pl.ds(0, n - 1)], recv_sem.at[kind])
        slot[...] = merge(recv1.at[kind], shares)
        for step in far_first(n):
            device = along(1 - kind, lax.rem(across + step, n))
            send(row, row, 9 + kind, device)
            send(slot, slot, 2 + kind, device)

    for kind in (1, 0):
        take(stat2.at[kind, pl.ds(0, n - 1)], recv_sem.at[9 + kind])
        shares, _ = shares_of(stat2.at[kind])
        slot = att.at[kind, mine[kind]]
        take(recv2.at[kind, pl.ds(0, n - 1)], recv_sem.at[2 + kind])
        slot[...] = merge(recv2.at[kind], shares)
        for step in far_first(n):
            device = along(kind, lax.rem(mine[kind] + step, n))
            send(slot, slot, 4 + kind, device)

    mixed = None
    for kind in (1, 0):
        take(att.at[kind, pl.ds(0, n - 1)], recv_sem.at[4 + kind])
        part = jnp.dot(
            wt_ref[:, kind * n * HALF : (kind + 1) * n * HALF],
            att[kind].reshape(n * HALF, rows),
            preferred_element_type=jnp.float32,
        )
        mixed = part if mixed is None else mixed + part
    send3[...] = mixed.T.reshape(send3.shape)
    for step in far_first(nk):
        to = lax.rem(kvh + step, nk)
        send(send3.at[to], recv3.at[kvh], 6, on_kvh(step))
    recv3[kvh] = send3[kvh]

    for kind in range(2):
        take(send1.at[kind, pl.ds(0, n - 1)], send_sem.at[kind])
        take(stat1.at[kind, pl.ds(0, n - 1)], send_sem.at[7 + kind])
        take(recv2.at[kind, pl.ds(0, n - 1)], send_sem.at[2 + kind])
        take(stat2.at[kind, pl.ds(0, n - 1)], send_sem.at[9 + kind])
        take(att.at[kind, pl.ds(0, n - 1)], send_sem.at[4 + kind])

    take(recv3.at[pl.ds(0, nk - 1)], recv_sem.at[6])
    out_ref[...] = jnp.sum(recv3[...], axis=0).astype(jnp.bfloat16)
    take(send3.at[pl.ds(0, nk - 1)], send_sem.at[6])


def solution(mesh):
    nk = mesh.shape["kvh"]
    n = math.isqrt(mesh.shape["ctx"])

    def step(queries, cache_keys, cache_values, lengths, w_out):
        rows, keys = queries.shape[0], cache_keys.shape[0]
        bf16, f32 = jnp.bfloat16, jnp.float32
        in_hbm = pl.BlockSpec(memory_space=pltpu.HBM)
        return pl.pallas_call(
            functools.partial(kernel, nk, n),
            out_shape=jax.ShapeDtypeStruct((rows // nk, HD), bf16),
            in_specs=[pl.BlockSpec(memory_space=pltpu.SMEM)] + [in_hbm] * 4,
            out_specs=pl.BlockSpec(memory_space=pltpu.VMEM),
            scratch_shapes=[
                pltpu.VMEM(queries.shape, bf16),
                pltpu.VMEM((keys, 2 * HD), bf16),
                pltpu.VMEM((keys, HD), bf16),
                pltpu.VMEM(w_out.shape, bf16),
                pltpu.VMEM((HD + ONE_ROWS, keys), bf16),
                pltpu.VMEM((HD, n * HD), bf16),
                pltpu.VMEM((2, keys, 2 * rows), f32),
                pltpu.VMEM((2, n, HALF, rows), bf16),
                pltpu.VMEM((2, n, HALF, rows), bf16),
                pltpu.VMEM((2, n, HALF, rows), bf16),
                pltpu.VMEM((2, n // 2, 1, rows), f32),
                pltpu.VMEM((2, n, 1, rows), f32),
                pltpu.VMEM((2, n, 1, rows), f32),
                pltpu.VMEM((2, n, HALF, rows), bf16),
                pltpu.VMEM((nk, rows // nk, HD), f32),
                pltpu.VMEM((nk, rows // nk, HD), f32),
                pltpu.SemaphoreType.DMA((4,)),
                pltpu.SemaphoreType.DMA((11,)),
                pltpu.SemaphoreType.DMA((11,)),
            ],
            compiler_params=pltpu.CompilerParams(
                collective_id=0, has_side_effects=True, vmem_limit_bytes=VMEM_BYTES
            ),
        )(lengths, queries, cache_keys, cache_values, w_out)

    in_specs = (P(None, "kvh"), P("ctx", "kvh"), P("ctx", "kvh"), P("ctx"), P("kvh", "ctx"))
    out_specs = P("kvh", "ctx")
    return jax.shard_map(step, mesh=mesh, in_specs=in_specs, out_specs=out_specs, check_vma=False)
```

```python
import functools
import math

import jax
import jax.numpy as jnp
from jax import lax
from jax.experimental import pallas as pl
from jax.experimental.pallas import tpu as pltpu
from jax.sharding import PartitionSpec as P

HD = 128
HALF = HD // 2
ONE_ROWS = 16
VMEM_BYTES = 53 * 2**20 + 800 * 2**10
MASKED = -1e30
SCALE = 1.0 / math.sqrt(HD)
LOG2E = math.log2(math.e)
MESH = pl.DeviceIdType.MESH


def shares_of(stats):
    rows = [stats[j] for j in range(stats.shape[0])]
    top = functools.reduce(jnp.maximum, rows)
    shares = [jnp.exp(row - top) for row in rows]
    total = functools.reduce(jnp.add, shares)
    scale = 1.0 / total
    return [share * scale for share in shares], top + jnp.log(total)


def merge(slots, shares):
    return functools.reduce(
        jnp.add,
        [slots[j].astype(jnp.float32) * share for j, share in enumerate(shares)],
    ).astype(jnp.bfloat16)


def far_first(n):
    return sorted(range(n - 1, 0, -1), key=lambda step: -min(step, n - step))


def kernel(
    nk, n,
    len_ref, q_hbm, k_hbm, v_hbm, w_hbm, out_ref,
    q_ref, k_ref, v_ref, w_ref, vt_ref, wt_ref, scores,
    send1, recv1, recv2, stat0, stat1, stat2, att, send3, recv3,
    load_sem, send_sem, recv_sem,
):
    rows = q_ref.shape[0]
    keys = k_ref.shape[0]
    pairs = n // 2
    kvh = lax.axis_index("kvh")
    ctx = lax.axis_index("ctx")
    y, z = ctx // n, lax.rem(ctx, n)
    mine = (y, z)

    load_k = pltpu.make_async_copy(k_hbm, k_ref.at[:, pl.ds(0, HD)], load_sem.at[0])
    load_q = pltpu.make_async_copy(q_hbm, q_ref, load_sem.at[1])
    load_v = pltpu.make_async_copy(v_hbm, v_ref, load_sem.at[2])
    load_w = pltpu.make_async_copy(w_hbm, w_ref, load_sem.at[3])
    load_k.start()
    load_q.start()
    load_v.start()
    load_w.start()

    def along(kind, to):
        return (kvh, to * n + z) if kind == 0 else (kvh, y * n + to)

    def on_kvh(step):
        return (lax.rem(kvh + step, nk), ctx)

    barrier = pltpu.get_barrier_semaphore()
    for step in far_first(n):
        for kind in range(2):
            device = along(kind, lax.rem(mine[kind] + step, n))
            pl.semaphore_signal(barrier, inc=1, device_id=device, device_id_type=MESH)
    for step in range(1, nk):
        pl.semaphore_signal(barrier, inc=1, device_id=on_kvh(step), device_id_type=MESH)

    def send(src, dst, index, device):
        pltpu.make_async_remote_copy(
            src_ref=src, dst_ref=dst, send_sem=send_sem.at[index],
            recv_sem=recv_sem.at[index], device_id=device, device_id_type=MESH,
        ).start()

    def take(ref, sem):
        pltpu.make_async_copy(ref, ref, sem).wait()

    lane = lax.broadcasted_iota(jnp.int32, (2 * rows, HD), 1)
    unit = jnp.where(lane == 0, 1.0, 0.0).astype(jnp.bfloat16)
    position = lax.broadcasted_iota(jnp.int32, (keys, HD), 0)
    column = lax.broadcasted_iota(jnp.int32, (keys, HD), 1)
    bias = jnp.where((column == 0) & (position >= len_ref[0]), MASKED, 0.0)
    k_ref[:, HD:] = bias.astype(jnp.bfloat16)

    orders = []
    for kind in range(2):
        place, odd = mine[kind] // 2, lax.rem(mine[kind], 2)
        steps = far_first(pairs) + [0]
        if pairs == 4:
            steps = [2, 1 + 2 * odd, 3 - 2 * odd, 0]
        orders.append([lax.rem(place + step, pairs) for step in steps])

    def give(kind, place, owner):
        device = along(kind, owner)
        send(stat0.at[kind, place], stat1.at[kind, mine[kind]], 7 + kind, device)
        send(send1.at[kind, owner], recv1.at[kind, mine[kind]], kind, device)

    def score(pair):
        heads = [orders[kind][pair] + kind * pairs for kind in range(2)]
        query = jnp.concatenate(
            [q_ref[:, pl.ds(pl.multiple_of(h * HD, HD), HD)] for h in heads], axis=0
        )
        query = jnp.concatenate([query, unit], axis=1)
        scores[pair % 2] = lax.dot_general(
            k_ref[...], query, (((1,), (1,)), ((), ())),
            preferred_element_type=jnp.float32,
        )

    load_q.wait()
    load_k.wait()
    score(0)
    load_v.wait()
    vt_ref[:HD] = v_ref[...].T
    vt_ref[HD:] = jnp.ones((ONE_ROWS, keys), jnp.bfloat16)
    for pair in range(pairs):
        if pair + 1 < pairs:
            score(pair + 1)
        block = scores[pair % 2]
        peak = jnp.max(block, axis=0, keepdims=True)
        weights = jnp.exp2((block - peak) * (SCALE * LOG2E)).astype(jnp.bfloat16)
        outs = jnp.dot(vt_ref[...], weights, preferred_element_type=jnp.float32)
        total = outs[HD : HD + 1]
        stat = peak * SCALE + jnp.log(total)
        outs = (outs[:HD] * (1.0 / total)).astype(jnp.bfloat16)
        if pair == 0:
            pl.semaphore_wait(barrier, 2 * (n - 1) + nk - 1)
        for kind in range(2):
            here = slice(kind * rows, (kind + 1) * rows)
            place = orders[kind][pair]
            stat0[kind, place] = stat[:, here]
            for half in range(2):
                owner = place * 2 + half
                send1[kind, owner] = outs[half * HALF : (half + 1) * HALF, here]
                if pair + 1 < pairs:
                    give(kind, place, owner)
            if pair + 1 == pairs:
                own = mine[kind]
                give(kind, place, own + 1 - 2 * lax.rem(own, 2))
                recv1[kind, own] = send1[kind, own]
                stat1[kind, own] = stat[:, here]

    load_w.wait()
    wt_ref[...] = w_ref[...].T

    for kind in range(2):
        take(stat1.at[kind, pl.ds(0, n - 1)], recv_sem.at[7 + kind])
        shares, stat = shares_of(stat1.at[kind])
        across = mine[1 - kind]
        row, slot = stat2.at[kind, across], recv2.at[kind, across]
        row[...] = stat
        take(recv1.at[kind, pl.ds(0, n - 1)], recv_sem.at[kind])
        slot[...] = merge(recv1.at[kind], shares)
        for step in far_first(n):
            device = along(1 - kind, lax.rem(across + step, n))
            send(row, row, 9 + kind, device)
            send(slot, slot, 2 + kind, device)

    for kind in (1, 0):
        take(stat2.at[kind, pl.ds(0, n - 1)], recv_sem.at[9 + kind])
        shares, _ = shares_of(stat2.at[kind])
        slot = att.at[kind, mine[kind]]
        take(recv2.at[kind, pl.ds(0, n - 1)], recv_sem.at[2 + kind])
        slot[...] = merge(recv2.at[kind], shares)
        for step in far_first(n):
            device = along(kind, lax.rem(mine[kind] + step, n))
            send(slot, slot, 4 + kind, device)

    mixed = None
    for kind in (1, 0):
        take(att.at[kind, pl.ds(0, n - 1)], recv_sem.at[4 + kind])
        part = jnp.dot(
            wt_ref[:, kind * n * HALF : (kind + 1) * n * HALF],
            att[kind].reshape(n * HALF, rows),
            preferred_element_type=jnp.float32,
        )
        mixed = part if mixed is None else mixed + part
    send3[...] = mixed.T.reshape(send3.shape)
    for step in far_first(nk):
        to = lax.rem(kvh + step, nk)
        send(send3.at[to], recv3.at[kvh], 6, on_kvh(step))
    recv3[kvh] = send3[kvh]

    for kind in range(2):
        take(send1.at[kind, pl.ds(0, n - 1)], send_sem.at[kind])
        take(stat1.at[kind, pl.ds(0, n - 1)], send_sem.at[7 + kind])
        take(recv2.at[kind, pl.ds(0, n - 1)], send_sem.at[2 + kind])
        take(stat2.at[kind, pl.ds(0, n - 1)], send_sem.at[9 + kind])
        take(att.at[kind, pl.ds(0, n - 1)], send_sem.at[4 + kind])

    take(recv3.at[pl.ds(0, nk - 1)], recv_sem.at[6])
    out_ref[...] = jnp.sum(recv3[...], axis=0).astype(jnp.bfloat16)
    take(send3.at[pl.ds(0, nk - 1)], send_sem.at[6])


def solution(mesh):
    nk = mesh.shape["kvh"]
    n = math.isqrt(mesh.shape["ctx"])

    def step(queries, cache_keys, cache_values, lengths, w_out):
        rows, keys = queries.shape[0], cache_keys.shape[0]
        bf16, f32 = jnp.bfloat16, jnp.float32
        in_hbm = pl.BlockSpec(memory_space=pltpu.HBM)
        return pl.pallas_call(
            functools.partial(kernel, nk, n),
            out_shape=jax.ShapeDtypeStruct((rows // nk, HD), bf16),
            in_specs=[pl.BlockSpec(memory_space=pltpu.SMEM)] + [in_hbm] * 4,
            out_specs=pl.BlockSpec(memory_space=pltpu.VMEM),
            scratch_shapes=[
                pltpu.VMEM(queries.shape, bf16),
                pltpu.VMEM((keys, 2 * HD), bf16),
                pltpu.VMEM((keys, HD), bf16),
                pltpu.VMEM(w_out.shape, bf16),
                pltpu.VMEM((HD + ONE_ROWS, keys), bf16),
                pltpu.VMEM((HD, n * HD), bf16),
                pltpu.VMEM((2, keys, 2 * rows), f32),
                pltpu.VMEM((2, n, HALF, rows), bf16),
                pltpu.VMEM((2, n, HALF, rows), bf16),
                pltpu.VMEM((2, n, HALF, rows), bf16),
                pltpu.VMEM((2, n // 2, 1, rows), f32),
                pltpu.VMEM((2, n, 1, rows), f32),
                pltpu.VMEM((2, n, 1, rows), f32),
                pltpu.VMEM((2, n, HALF, rows), bf16),
                pltpu.VMEM((nk, rows // nk, HD), f32),
                pltpu.VMEM((nk, rows // nk, HD), f32),
                pltpu.SemaphoreType.DMA((4,)),
                pltpu.SemaphoreType.DMA((11,)),
                pltpu.SemaphoreType.DMA((11,)),
            ],
            compiler_params=pltpu.CompilerParams(
                collective_id=0, has_side_effects=True, vmem_limit_bytes=VMEM_BYTES
            ),
        )(lengths, queries, cache_keys, cache_values, w_out)

    in_specs = (P(None, "kvh"), P("ctx", "kvh"), P("ctx", "kvh"), P("ctx"), P("kvh", "ctx"))
    out_specs = P("kvh", "ctx")
    return jax.shard_map(step, mesh=mesh, in_specs=in_specs, out_specs=out_specs, check_vma=False)
```
